32 devices in a mesh: dp: 8 (over z, x), head: 4 (over y, core).
Axes of the slice: x: 2, y: 2, z: 4, core: 2. Of those that a mesh axis runs over, the one named last changes fastest.
Arguments:
- tokens: bfloat16 [4096, 4096], P('dp'), may hold values from -6 to 6
- q_weight: bfloat16 [4096, 8192], P('dp', 'head'), may hold values from -0.09375 to 0.09375
- kv_weight: bfloat16 [4096, 1024], P('dp', 'head'), may hold values from -0.09375 to 0.09375
- q_gain: float32 [128], replicated, may hold values from 0.1 to 1.9
- k_gain: float32 [128], replicated, may hold values from 0.1 to 1.9
- doc_lengths: int32 [8, 16], replicated, may hold values from 0 to 512, as said below
Outputs:
- attended: bfloat16 [4096, 8192], P('dp', 'head')
The draws below stay inside these ranges and needn't reach their ends.
Inputs may be any that keep to these rules, and one draw needn't show every extreme that they name: `doc_lengths`: row r lists the lengths of the documents packed in order on index r of dp and sums to 512; some rank holds a single document of 512 tokens.
All inputs are finite; a program needn't handle non-finite values.
Results may differ from the reference program's by a relative error of at most 0.0068.
Values may be sent and summed in bfloat16 or wider, within the bound.
No kernel may reach another device: no remote copies, remote signals or barrier semaphores. Data moves between devices by JAX's collectives and lax.ppermute only.
A program may use at most 64 MiB of HBM per device.

```python
import math
import jax
import jax.numpy as jnp
from jax import lax

D = 4096
QH = 64
KVH = 4
HD = 128
TOK_DEV = 512
NDOC = 16
TOKENS = 4096
N_DP = 8


def draw_doc_lengths(key, part):
    key_count, key_weight, key_rank = jax.random.split(jax.random.fold_in(key, 7), 3)
    rank_ids = jnp.arange(N_DP, dtype=jnp.int32)
    doc_count = jax.random.randint(key_count, (N_DP, 1), 1, NDOC + 1)
    single_rank = jax.random.randint(key_rank, (), 0, N_DP)
    doc_count = jnp.where(rank_ids[:, None] == single_rank, 1, doc_count)
    weights = jax.random.randint(key_weight, (N_DP, NDOC), 1, 9)
    weights = jnp.where(jnp.arange(NDOC, dtype=jnp.int32)[None, :] < doc_count, weights, 0)
    weight_sum = jnp.sum(weights, axis=1, keepdims=True)
    lengths = weights * TOK_DEV // weight_sum
    shortfall = TOK_DEV - jnp.sum(lengths, axis=1, keepdims=True)
    lengths = jnp.where(jnp.arange(NDOC, dtype=jnp.int32)[None, :] == 0, lengths + shortfall, lengths)
    return lengths.astype(jnp.int32)


def block_scale(stream_key, extent, cuts, low, high):
    def one(dim, shards_of):
        draws = jax.random.uniform(jax.random.fold_in(jax.random.fold_in(stream_key, 6), dim), (shards_of,), jnp.float32, low / len(cuts), high / len(cuts))
        return jnp.repeat(jnp.exp(draws), extent[dim] // shards_of).reshape((-1,) + (1,) * (len(extent) - dim - 1))

    loudness = one(*cuts[0])
    for cut in cuts[1:]:
        loudness = loudness * one(*cut)
    return loudness


def normal_values(stream_key, shape, scale, reach, shards=(), held_as=jnp.bfloat16):
    loudness = block_scale(stream_key, shape, shards, -0.22, 0.18) if shards else 1.0
    drawn = jax.random.normal(stream_key, shape, jnp.float32) * scale * loudness
    return jnp.minimum(jnp.maximum(drawn, -reach), reach).astype(held_as)


def setup_inputs(seed: int = 0) -> dict:
    splits = jax.random.split(jax.random.key(seed), 7)
    return {
        "tokens": normal_values(splits[0], (TOKENS, D), 1.0, 6.0, ((0, 8),)),
        "q_weight": normal_values(splits[1], (D, QH * HD), D ** -0.5, 0.09375, ((0, 8), (1, 4))),
        "kv_weight": normal_values(splits[2], (D, 2 * KVH * HD), D ** -0.5, 0.09375, ((0, 8), (1, 4))),
        "q_gain": jnp.clip(1.0 + 0.18 * jax.random.normal(splits[3], (HD,), jnp.float32), 0.1, 1.9),
        "k_gain": jnp.clip(1.0 + 0.18 * jax.random.normal(splits[4], (HD,), jnp.float32), 0.1, 1.9),
        "doc_lengths": draw_doc_lengths(jax.random.fold_in(splits[6], 71), 0),
    }


theta_base = 1000000.0
norm_eps = 1e-06

def doc_layout(lengths, count):
    doc_ends = jnp.cumsum(lengths).astype(jnp.int32)
    places = jnp.arange(count, dtype=jnp.int32)
    passed = (places[:, None] >= doc_ends[None, :]).astype(jnp.int32)
    doc_ids = lax.optimization_barrier(jnp.sum(passed, axis=1)).astype(jnp.int32)
    starts = lax.optimization_barrier(jnp.sum(passed * lengths[None, :], axis=1)).astype(jnp.int32)
    return (doc_ids, places - starts)

def norm_rope(raw, gain, positions):
    half_width = raw.shape[-1] // 2
    inv_rms = lax.rsqrt(lax.optimization_barrier(jnp.mean(raw * raw, axis=-1, keepdims=True)) + norm_eps)
    normed = raw * inv_rms * gain
    frequency = jnp.exp(jnp.arange(half_width, dtype=jnp.float32) * (-2.0 * math.log(theta_base) / raw.shape[-1]))
    angles = positions.astype(jnp.float32)[:, None] * frequency[None, :]
    cosine = jnp.cos(angles)[:, None, :]
    sine_table = jnp.sin(angles)[:, None, :]
    lower_half = normed[..., :half_width]
    second = normed[..., half_width:]
    return jnp.concatenate([lower_half * cosine - second * sine_table, second * cosine + lower_half * sine_table], axis=-1).astype(jnp.bfloat16)

def reference(tokens, q_weight, kv_weight, q_gain, k_gain, doc_lengths):
    head_group = QH // KVH

    def one_rank(rank_index):
        token_rows = lax.dynamic_slice_in_dim(tokens, rank_index * TOK_DEV, TOK_DEV, 0)
        lengths = lax.dynamic_index_in_dim(doc_lengths, rank_index, 0, keepdims=False)
        doc_ids, positions = doc_layout(lengths, TOK_DEV)
        places = jnp.arange(TOK_DEV, dtype=jnp.int32)
        q_raw = jnp.dot(token_rows, q_weight, preferred_element_type=jnp.float32).reshape(TOK_DEV, QH, HD)
        kv_raw = jnp.dot(token_rows, kv_weight, preferred_element_type=jnp.float32)
        k_raw = kv_raw[:, :KVH * HD].reshape(TOK_DEV, KVH, HD)
        values = kv_raw[:, KVH * HD:].reshape(TOK_DEV, KVH, HD).astype(jnp.bfloat16)
        queries = norm_rope(q_raw, q_gain, positions).reshape(TOK_DEV, KVH, head_group, HD)
        key_rows = norm_rope(k_raw, k_gain, positions)
        scores = jnp.einsum('qkgd,tkd->kgqt', queries.astype(jnp.float32), key_rows.astype(jnp.float32)) * HD ** (-0.5)
        allowed = (doc_ids[:, None] == doc_ids[None, :]) & (places[:, None] >= places[None, :])
        weights = jnp.where(allowed[None, None], jnp.exp(scores), 0.0)
        weights_bf = (weights / lax.optimization_barrier(jnp.sum(weights, axis=-1, keepdims=True))).astype(jnp.bfloat16)
        mixed_out = jnp.einsum('kgqt,tkd->qkgd', weights_bf.astype(jnp.float32), values.astype(jnp.float32))
        return mixed_out.astype(jnp.bfloat16).reshape(TOK_DEV, QH * HD)
    stacked = lax.map(one_rank, jnp.arange(N_DP, dtype=jnp.int32))
    return stacked.reshape(TOK_DEV * N_DP, QH * HD)
```

```python
import functools
import math

import jax
import jax.numpy as jnp
from jax import lax
from jax.experimental import pallas as pl
from jax.experimental.pallas import tpu as pltpu
from jax.sharding import PartitionSpec as P

KVH = 4
HD = 128


theta_base = 1000000.0
norm_eps = 1e-06

CHUNK_SHARES = (4, 4, 4, 4)
KV_WITH = 1


def doc_starts(lengths, count):
    doc_ends = jnp.cumsum(lengths)
    places = jnp.arange(count, dtype=jnp.int32)
    passed = (places[:, None] >= doc_ends[None, :]).astype(jnp.int32)
    return jnp.sum(passed * lengths[None, :], axis=1)


def rope_tables(positions):
    half_width = HD // 2
    frequency = jnp.exp(
        jnp.arange(half_width, dtype=jnp.float32) * (-2.0 * math.log(theta_base) / HD)
    )
    angles = positions.astype(jnp.float32)[:, None] * frequency[None, :]
    cosine, sine = jnp.cos(angles), jnp.sin(angles)
    return (
        jnp.concatenate([cosine, cosine], axis=1),
        jnp.concatenate([-sine, sine], axis=1),
    )


def norm_rope(raw, gain, cosine, sine, swap_halves):
    inv_rms = lax.rsqrt(jnp.mean(raw * raw, axis=-1, keepdims=True) + norm_eps)
    normed = raw * inv_rms * gain
    return (normed * cosine + swap_halves(normed) * sine).astype(jnp.bfloat16)


def attend_kernel(block, mine, other, keys, values, cosine, sine, starts, gain, out):
    rows = mine.shape[0]
    raw = mine[...] + other[...].astype(jnp.float32)
    queries = norm_rope(
        raw, gain[...], cosine[...], sine[...], lambda n: pltpu.roll(n, HD // 2, 1)
    )
    for first in range(0, rows, block):
        here, upto = slice(first, first + block), first + block
        scores = lax.dot_general(
            queries[here], keys[:upto, :], (((1,), (1,)), ((), ())),
            preferred_element_type=jnp.float32,
        ) * HD ** (-0.5)
        col = lax.broadcasted_iota(jnp.int32, scores.shape, 1)
        row = lax.broadcasted_iota(jnp.int32, scores.shape, 0) + first
        allowed = (col >= starts[here, :]) & (col <= row)
        weights = jnp.where(allowed, jnp.exp(scores), 0.0)
        probs = (weights / jnp.sum(weights, axis=-1, keepdims=True)).astype(jnp.bfloat16)
        mixed = jnp.dot(probs, values[:upto, :], preferred_element_type=jnp.float32)
        out[here, :] = mixed.astype(out.dtype)


def attend(mine, other, keys, values, cosine, sine, starts, gain):
    rows, cols = mine.shape
    block = 128 if rows % 128 == 0 else rows
    by_head = pl.BlockSpec((rows, HD), lambda h: (0, h))
    whole = lambda a: pl.BlockSpec(a.shape, lambda h: (0, 0))
    return pl.pallas_call(
        functools.partial(attend_kernel, block),
        grid=(cols // HD,),
        out_shape=jax.ShapeDtypeStruct((rows, cols), jnp.bfloat16),
        in_specs=[by_head, by_head] + [whole(a) for a in (keys, values, cosine, sine, starts, gain)],
        out_specs=by_head,
        compiler_params=pltpu.CompilerParams(vmem_limit_bytes=32 << 20),
        cost_estimate=pl.CostEstimate(
            flops=4 * rows * rows * cols, bytes_accessed=8 * rows * cols,
            transcendentals=rows * rows * cols // HD,
        ),
        name="attend",
    )(mine, other, keys, values, cosine, sine, starts, gain)


def shards(tokens, q_weight, kv_weight, q_gain, k_gain, doc_lengths):
    rows, depth = tokens.shape[0], q_weight.shape[0]
    cols = q_weight.shape[1]
    n_dp, n_head = lax.axis_size("dp"), lax.axis_size("head")
    n_line = n_dp // 2
    n_pairs = n_line // 2
    rank, head = lax.axis_index("dp"), lax.axis_index("head")
    spot, side = rank // 2, rank % 2
    pair = spot // 2

    hub_of = lambda g: 2 * g + 1 if 2 * g < n_pairs else 2 * g
    hub_bit = jnp.where(2 * pair < n_pairs, 1, 0)
    is_hub = spot % 2 == hub_bit

    def on_line(moves):
        return [(2 * a + s, 2 * b + s) for a, b in moves for s in range(2)]

    swap = on_line([(a, a ^ 1) for a in range(n_line)])
    shift = [
        on_line([(hub_of(g), hub_of((g + s) % n_pairs)) for g in range(n_pairs)])
        for s in range(n_pairs)
    ]
    outward = on_line([(hub_of(g), hub_of(g) ^ 1) for g in range(n_pairs)])
    across = [(a, a ^ 1) for a in range(n_dp)]
    send = lambda value, moves: lax.ppermute(value, "dp", moves)

    order = [spot, spot ^ 1]
    for s in range(1, n_pairs):
        source = (pair - s + n_pairs) % n_pairs
        hub = 2 * source + jnp.where(2 * source < n_pairs, 1, 0)
        order += [hub, hub ^ 1]

    def features(block, of_side):
        return [
            lax.dynamic_slice_in_dim(block, (2 * at + of_side) * depth, depth, 1) for at in order
        ]

    share = rows // n_head
    quarter = lax.dynamic_slice_in_dim(tokens, head * share, share, 0)
    own_tokens = features(tokens, side)
    their_quarter = send(jnp.concatenate(features(quarter, 1 - side), axis=1), across)
    their_tokens = lax.all_gather(their_quarter, "head", axis=0, tiled=True)

    kv_all = lax.all_gather(kv_weight, "head", axis=1, tiled=True)
    kv_head = head * KVH // n_head
    kv_cols = jnp.concatenate(
        [
            lax.dynamic_slice_in_dim(kv_all, kv_head * HD, HD, 1),
            lax.dynamic_slice_in_dim(kv_all, (KVH + kv_head) * HD, HD, 1),
        ],
        axis=1,
    )

    def gather(piece):
        pieces = [piece, send(piece, swap)]
        for s in range(1, n_pairs):
            for part in pieces[:2]:
                inward = send(part, shift[s])
                pieces.append(jnp.where(is_hub, inward, send(inward, outward)))
        return pieces

    def half_sums(pieces):
        mine = sum(
            jnp.dot(t, w, preferred_element_type=jnp.float32)
            for t, w in zip(own_tokens, pieces, strict=True)
        )
        theirs = sum(
            jnp.dot(their_tokens[:, i * depth : (i + 1) * depth], w, preferred_element_type=jnp.float32)
            for i, w in enumerate(pieces)
        )
        return mine, theirs

    lengths = lax.dynamic_index_in_dim(doc_lengths, rank, 0, keepdims=False)
    starts = doc_starts(lengths, rows)
    cosine, sine = rope_tables(jnp.arange(rows, dtype=jnp.int32) - starts)

    heads = cols // HD
    bounds, taken = [], 0
    for part in CHUNK_SHARES:
        count = part * heads // sum(CHUNK_SHARES)
        bounds.append((taken * HD, (taken + count) * HD))
        taken += count
    sums = []
    for j, (low, high) in enumerate(bounds):
        piece = q_weight[:, low:high]
        if j == KV_WITH:
            piece = jnp.concatenate([piece, kv_cols], axis=1)
        mine, theirs = half_sums(gather(piece))
        width = high - low
        if j == KV_WITH:
            kv = mine[:, width:] + send(theirs[:, width:], across)
            mine, theirs = mine[:, :width], theirs[:, :width]
        sums.append((mine, send(theirs.astype(jnp.bfloat16), across)))
    keys = norm_rope(
        kv[:, :HD], k_gain, cosine, sine,
        lambda n: jnp.concatenate([n[:, HD // 2 :], n[:, : HD // 2]], axis=1),
    )
    values = kv[:, HD:].astype(jnp.bfloat16)
    parts = [
        attend(mine, other, keys, values, cosine, sine, starts[:, None], q_gain[None, :])
        for mine, other in sums
    ]
    return jnp.concatenate(parts, axis=1)


def solution(mesh):
    placed = (P("dp", None), P("dp", "head"), P("dp", "head"), P(), P(), P())
    return jax.shard_map(
        shards, mesh=mesh, in_specs=placed, out_specs=P("dp", "head"), check_vma=False
    )
```

```python
import functools
import math

import jax
import jax.numpy as jnp
from jax import lax
from jax.experimental import pallas as pl
from jax.experimental.pallas import tpu as pltpu
from jax.sharding import PartitionSpec as P

KVH = 4
HD = 128


theta_base = 1000000.0
norm_eps = 1e-06

RUNS = (3, 2, 4, 3, 3, 1)


def doc_starts(lengths, count):
    doc_ends = jnp.cumsum(lengths)
    places = jnp.arange(count, dtype=jnp.int32)
    passed = (places[:, None] >= doc_ends[None, :]).astype(jnp.int32)
    return jnp.sum(passed * lengths[None, :], axis=1)


def rope_tables(positions):
    half_width = HD // 2
    frequency = jnp.exp(
        jnp.arange(half_width, dtype=jnp.float32) * (-2.0 * math.log(theta_base) / HD)
    )
    angles = positions.astype(jnp.float32)[:, None] * frequency[None, :]
    cosine, sine = jnp.cos(angles), jnp.sin(angles)
    return (
        jnp.concatenate([cosine, cosine], axis=1),
        jnp.concatenate([-sine, sine], axis=1),
    )


def norm_rope(raw, gain, cosine, sine, swap_halves):
    inv_rms = lax.rsqrt(jnp.mean(raw * raw, axis=-1, keepdims=True) + norm_eps)
    normed = raw * inv_rms * gain
    return (normed * cosine + swap_halves(normed) * sine).astype(jnp.bfloat16)


def attend_kernel(block, mine, other, keys, values, cosine, sine, starts, gain, out):
    rows, cols = mine.shape
    heads = [slice(low, low + HD) for low in range(0, cols, HD)]
    queries = [
        norm_rope(
            mine[:, at] + other[:, at].astype(jnp.float32), gain[...], cosine[...], sine[...],
            lambda n: pltpu.roll(n, HD // 2, 1),
        )
        for at in heads
    ]
    for first in range(0, rows, block):
        here, upto = slice(first, first + block), first + block
        col = lax.broadcasted_iota(jnp.int32, (block, upto), 1)
        row = lax.broadcasted_iota(jnp.int32, (block, upto), 0) + first
        allowed = (col >= starts[here, :]) & (col <= row)
        scores = [
            lax.dot_general(
                q[here], keys[:upto, :], (((1,), (1,)), ((), ())),
                preferred_element_type=jnp.float32,
            )
            for q in queries
        ]
        weights = [
            jnp.where(allowed, jnp.exp2(s * (HD**-0.5 * math.log2(math.e))), 0.0) for s in scores
        ]
        probs = [
            (w * (1.0 / jnp.sum(w, axis=-1, keepdims=True))).astype(jnp.bfloat16) for w in weights
        ]
        for at, p in zip(heads, probs, strict=True):
            mixed = jnp.dot(p, values[:upto, :], preferred_element_type=jnp.float32)
            out[here, at] = mixed.astype(out.dtype)


def attend(mine, other, keys, values, cosine, sine, starts, gain):
    rows, cols = mine.shape
    block = 128 if rows % 128 == 0 else rows
    heads = cols // HD
    step = max(n for n in range(1, 5) if heads % n == 0) * HD
    by_heads = pl.BlockSpec((rows, step), lambda h: (0, h))
    whole = lambda a: pl.BlockSpec(a.shape, lambda h: (0, 0))
    return pl.pallas_call(
        functools.partial(attend_kernel, block),
        grid=(cols // step,),
        out_shape=jax.ShapeDtypeStruct((rows, cols), jnp.bfloat16),
        in_specs=[by_heads, by_heads]
        + [whole(a) for a in (keys, values, cosine, sine, starts, gain)],
        out_specs=by_heads,
        compiler_params=pltpu.CompilerParams(vmem_limit_bytes=24 << 20),
        cost_estimate=pl.CostEstimate(flops=0, bytes_accessed=0, transcendentals=0),
        name="attend",
    )(mine, other, keys, values, cosine, sine, starts, gain)


def product_kernel(depth, windows, count, flag, tokens, *refs):
    out, arrays = refs[-1], refs[:-1]
    cols = out.shape[1]

    def add_up(which):
        total = jnp.zeros(out.shape, jnp.float32)
        for i, (at, low) in enumerate(which):
            total += jnp.dot(
                tokens[:, i * depth : (i + 1) * depth], arrays[at][:, low : low + cols],
                preferred_element_type=jnp.float32,
            )
        out[...] = total.astype(out.dtype)

    if len(windows) == count:
        add_up(windows)
    else:
        pl.when(flag[0] == 1)(lambda: add_up(windows[:count]))
        pl.when(flag[0] == 0)(lambda: add_up(windows[count:]))


def product(is_hub, tokens, cols, at_hub, at_leaf, dtype):
    rows, depth = tokens.shape[0], at_hub[0][0].shape[0]
    arrays, windows = [], []
    for array, low in [*at_hub, *(at_leaf or [])]:
        known = [i for i, a in enumerate(arrays) if a is array]
        if not known:
            arrays.append(array)
        windows.append((known[0] if known else len(arrays) - 1, low))
    block = 256 if rows % 256 == 0 else rows
    return pl.pallas_call(
        functools.partial(product_kernel, depth, tuple(windows), len(at_hub)),
        grid=(rows // block,),
        out_shape=jax.ShapeDtypeStruct((rows, cols), dtype),
        in_specs=[pl.BlockSpec(memory_space=pltpu.SMEM), pl.BlockSpec((block, tokens.shape[1]), lambda r: (r, 0))]
        + [pl.BlockSpec(p.shape, lambda r: (0, 0), pipeline_mode=pl.Buffered(1)) for p in arrays],
        out_specs=pl.BlockSpec((block, cols), lambda r: (r, 0)),
        compiler_params=pltpu.CompilerParams(vmem_limit_bytes=24 << 20),
        cost_estimate=pl.CostEstimate(flops=0, bytes_accessed=0, transcendentals=0),
        name="product",
    )(is_hub.astype(jnp.int32)[None], tokens, *arrays)


def kv_columns(kv_weight, head, n_head):
    if n_head == KVH:
        halves = kv_weight[:, :HD], kv_weight[:, HD:]
        has_keys = head < n_head // 2
        first = lax.ppermute(
            jnp.where(has_keys, *halves), "head",
            [(a, 2 * a) if 2 * a < n_head else (a, 2 * a - n_head + 1) for a in range(n_head)],
        )
        second = lax.ppermute(
            jnp.where(has_keys, *halves[::-1]), "head",
            [(a, 2 * a + 1) if 2 * a < n_head else (a, 2 * a - n_head) for a in range(n_head)],
        )
        even = head % 2 == 0
        return [jnp.where(even, first, second), jnp.where(even, second, first)]
    kv_all = lax.all_gather(kv_weight, "head", axis=1, tiled=True)
    kv_head = head * KVH // n_head
    return [
        lax.dynamic_slice_in_dim(kv_all, (part * KVH + kv_head) * HD, HD, 1) for part in range(2)
    ]


def after(value, *others):
    return lax.optimization_barrier((value, *others))[0]


def split_shares(heads, shares):
    total, bounds, sofar = sum(shares), [], 0
    for share in shares:
        bounds.append((sofar * heads // total * HD, (sofar + share) * heads // total * HD))
        sofar += share
    return bounds


def shards(tokens, q_weight, kv_weight, q_gain, k_gain, doc_lengths):
    rows, depth = tokens.shape[0], q_weight.shape[0]
    heads = q_weight.shape[1] // HD
    n_dp, n_head = lax.axis_size("dp"), lax.axis_size("head")
    n_line = n_dp // 2
    n_pairs = n_line // 2
    rank, head = lax.axis_index("dp"), lax.axis_index("head")
    spot, side = rank // 2, rank % 2
    pair = spot // 2

    hub_of = lambda g: 2 * g + 1 if 2 * g < n_pairs else 2 * g
    is_hub = spot % 2 == jnp.where(2 * pair < n_pairs, 1, 0)

    def on_line(moves):
        return [(2 * a + s, 2 * b + s) for a, b in moves for s in range(2)]

    swap = on_line([(a, a ^ 1) for a in range(n_line)])
    outward = on_line([(hub_of(g), hub_of(g) ^ 1) for g in range(n_pairs)])
    across = [(a, a ^ 1) for a in range(n_dp)]
    send = lambda value, moves: lax.ppermute(value, "dp", moves)

    def round_hubs(part):
        return [
            send(part, on_line([(hub_of(g), hub_of((g + s) % n_pairs)) for g in range(n_pairs)]))
            for s in range(1, n_pairs)
        ]

    def to_leaf(parts):
        return [send(part, outward) for part in parts]

    def woven(own, partners, hubs, leaves):
        return [own, partners] + [p for two in zip(hubs, leaves, strict=True) for p in two]

    order = [spot, spot ^ 1]
    for s in range(1, n_pairs):
        source = (pair - s + n_pairs) % n_pairs
        hub = 2 * source + jnp.where(2 * source < n_pairs, 1, 0)
        order += [hub, hub ^ 1]

    def features(block, of_side):
        return jnp.concatenate(
            [lax.dynamic_slice_in_dim(block, (2 * at + of_side) * depth, depth, 1) for at in order],
            axis=1,
        )

    def tables(of_rank):
        lengths = lax.dynamic_index_in_dim(doc_lengths, of_rank, 0, keepdims=False)
        starts = doc_starts(lengths, rows)
        return (*rope_tables(jnp.arange(rows, dtype=jnp.int32) - starts), starts[:, None])

    even = head % 2 == 0
    twins = [(a, a ^ 1) for a in range(n_head)]
    share = rows // 2
    part = lax.dynamic_slice_in_dim(tokens, head % 2 * share, share, 0)
    part = send(features(part, 1 - side), across)
    twin = lax.ppermute(part, "head", twins)
    beside_tokens = jnp.concatenate(
        [jnp.where(even, part, twin), jnp.where(even, twin, part)], axis=0
    )
    own_tokens = features(tokens, side)
    cosine, sine, starts = tables(rank)

    bounds = [b for b in split_shares(heads, RUNS) if b[0] < b[1]]
    count = len(bounds)
    widths = [high - low for low, high in bounds]
    with_kv = 1
    wides = [w + (2 * HD if k == with_kv else 0) for k, w in enumerate(widths)]
    owns = [q_weight[:, : bounds[0][1]]]
    first = send(owns[0], swap)
    kv_cols = kv_columns(after(kv_weight, owns[0]), head, n_head)
    owns.append(q_weight[:, bounds[1][0] : bounds[1][1]])
    late_weight = after(q_weight, first)
    owns += [late_weight[:, low:high] for low, high in bounds[2:]]
    owns[with_kv] = jnp.concatenate([owns[with_kv], *kv_cols], axis=1)
    cut = lambda k, where: where[0][:, where[1] : where[1] + wides[k]]
    joined = lambda blocks: jnp.concatenate(blocks, axis=1) if len(blocks) > 1 else blocks[0]

    got, hub_at, leaf_at = {}, {}, {}

    def go_round(k, *ties):
        blocks, taken = [], []
        if k + 2 < count:
            blocks.append(owns[k + 2])
            taken.append((hub_at, k + 2, 0))
        if 0 <= k + 1 < count:
            taken.append((leaf_at, k + 1, sum(b.shape[1] for b in blocks)))
            blocks.append(cut(k + 1, got[k + 1]))
        if blocks:
            moved = round_hubs(after(joined(blocks), *ties))
            for table, run, low in taken:
                table[run] = [(p, low) for p in moved]

    got[0] = (first, 0)
    go_round(-2)
    second = send(joined([after(owns[1], first, *[p for p, _ in hub_at[0]])] + owns[2:3]), swap)
    got[1], got[2] = (second, 0), (second, wides[1])
    go_round(-1)
    go_round(0)

    exchanged, sums, parts, computed = [first, second], [], [], {}
    keys = None
    for k in range(count):
        blocks = [owns[k + 3]] if k + 3 < count else []
        low = wides[k + 3] if blocks else 0
        blocks += [cut(k, w) for h, l in zip(hub_at[k], leaf_at[k], strict=True) for w in (h, l)]
        ties = [exchanged[-2]] + computed.get(k - 3, [])
        passed = send(after(joined(blocks), *ties), swap)
        exchanged.append(passed)
        if k + 3 < count:
            got[k + 3] = (passed, 0)
        if k + 1 < count:
            go_round(k + 1, exchanged[-2])
        wide = wides[k]
        at_leaf = [own_at for own_at in [(owns[k], 0), got[k]]]
        at_leaf += [(passed, low + i * wide) for i in range(2 * (n_pairs - 1))]
        pieces = woven((owns[k], 0), got[k], hub_at[k], leaf_at[k]), at_leaf
        theirs = product(
            is_hub, after(beside_tokens, *computed.get(k - 1, [])), wide, *pieces, jnp.float32 if k == with_kv else jnp.bfloat16
        )
        if k == with_kv:
            other_kv = send(theirs[:, widths[k] :], across)
            theirs = theirs[:, : widths[k]].astype(jnp.bfloat16)
        other = send(theirs, across)
        mine = product(is_hub, own_tokens, wide, *pieces, jnp.float32)
        if k == with_kv:
            kv = mine[:, widths[k] :] + other_kv
            mine = mine[:, : widths[k]]
            keys = norm_rope(
                kv[:, :HD], k_gain, cosine, sine,
                lambda n: jnp.concatenate([n[:, HD // 2 :], n[:, : HD // 2]], axis=1),
            )
            values = kv[:, HD:].astype(jnp.bfloat16)
        sums.append((mine, other))
        computed[k] = [mine]
        if keys is not None:
            late = 1
            while len(parts) < len(sums) - late:
                parts.append(
                    attend(*sums[len(parts)], keys, values, cosine, sine, starts, q_gain[None, :])
                )
                computed[k].append(parts[-1])
    parts.append(attend(*sums[-1], keys, values, cosine, sine, starts, q_gain[None, :]))
    return jnp.concatenate(parts, axis=1)


def solution(mesh):
    placed = (P("dp", None), P("dp", "head"), P("dp", "head"), P(), P(), P())
    return jax.shard_map(
        shards, mesh=mesh, in_specs=placed, out_specs=P("dp", "head"), check_vma=False
    )
```

```python
import functools
import math

import jax
import jax.numpy as jnp
from jax import lax
from jax.experimental import pallas as pl
from jax.experimental.pallas import tpu as pltpu
from jax.sharding import PartitionSpec as P

KVH = 4
HD = 128


theta_base = 1000000.0
norm_eps = 1e-06

RUNS = (4, 3, 4, 4, 1)


def doc_starts(lengths, count):
    doc_ends = jnp.cumsum(lengths)
    places = jnp.arange(count, dtype=jnp.int32)
    passed = (places[:, None] >= doc_ends[None, :]).astype(jnp.int32)
    return jnp.sum(passed * lengths[None, :], axis=1)


def rope_tables(positions, starts):
    half_width = HD // 2
    frequency = jnp.exp(
        jnp.arange(half_width, dtype=jnp.float32) * (-2.0 * math.log(theta_base) / HD)
    )
    angles = positions.astype(jnp.float32)[:, None] * frequency[None, :]
    cosine, sine = jnp.cos(angles), jnp.sin(angles)
    wide_starts = jnp.broadcast_to(starts.astype(jnp.float32)[:, None], (starts.shape[0], HD))
    return jnp.concatenate([cosine, cosine, -sine, sine, wide_starts], axis=1)


def norm_rope(raw, gain, cosine, sine, swap_halves):
    inv_rms = lax.rsqrt(jnp.mean(raw * raw, axis=-1, keepdims=True) + norm_eps)
    normed = raw * inv_rms * gain
    return (normed * cosine + swap_halves(normed) * sine).astype(jnp.bfloat16)


def attend_kernel(block, mine, other, keys_values, tables, gain, out):
    rows, cols = mine.shape
    heads = [slice(low, low + HD) for low in range(0, cols, HD)]
    keys, values = keys_values.at[:, :HD], keys_values.at[:, HD:]
    queries = [
        norm_rope(
            mine[:, at] + other[:, at].astype(jnp.float32), gain[...], tables[:, :HD],
            tables[:, HD : 2 * HD], lambda n: pltpu.roll(n, HD // 2, 1),
        )
        for at in heads
    ]
    for first in range(0, rows, block):
        here, upto = slice(first, first + block), first + block
        col = lax.broadcasted_iota(jnp.int32, (block, upto), 1)
        row = lax.broadcasted_iota(jnp.int32, (block, upto), 0) + first
        starts = tables[here, 2 * HD : 2 * HD + 1].astype(jnp.int32)
        allowed = (col >= starts) & (col <= row)
        scores = [
            lax.dot_general(
                q[here], keys[:upto, :], (((1,), (1,)), ((), ())),
                preferred_element_type=jnp.float32,
            )
            for q in queries
        ]
        weights = [
            jnp.where(allowed, jnp.exp2(s * (HD**-0.5 * math.log2(math.e))), 0.0) for s in scores
        ]
        probs = [
            (w * (1.0 / jnp.sum(w, axis=-1, keepdims=True))).astype(jnp.bfloat16) for w in weights
        ]
        for at, p in zip(heads, probs, strict=True):
            mixed = jnp.dot(p, values[:upto, :], preferred_element_type=jnp.float32)
            out[here, at] = mixed.astype(out.dtype)


def attend(mine, other, keys_values, tables, gain):
    rows, cols = mine.shape
    block = 128 if rows % 128 == 0 else rows
    heads = cols // HD
    step = max(n for n in range(1, 5) if heads % n == 0) * HD
    by_heads = pl.BlockSpec((rows, step), lambda h: (0, h))
    whole = lambda a: pl.BlockSpec(a.shape, lambda h: (0, 0))
    return pl.pallas_call(
        functools.partial(attend_kernel, block),
        grid=(cols // step,),
        out_shape=jax.ShapeDtypeStruct((rows, cols), jnp.bfloat16),
        in_specs=[by_heads, by_heads] + [whole(a) for a in (keys_values, tables, gain)],
        out_specs=by_heads,
        compiler_params=pltpu.CompilerParams(vmem_limit_bytes=24 << 20),
        cost_estimate=pl.CostEstimate(flops=0, bytes_accessed=0, transcendentals=0),
        name="attend",
    )(mine, other, keys_values, tables, gain)


def product_kernel(windows, count, sides, flag, *refs):
    tokens, arrays, outs = refs[:sides], refs[sides : -sides - 3], refs[-sides - 3 : -3]
    features, weights, arrived = refs[-3:]
    depth, cols = weights.shape[1:]
    rows = tokens[0].shape[0]
    block = 256 if rows % 256 == 0 else rows

    def rows_of(which, i):
        at, low = which[i]
        return pltpu.make_async_copy(
            arrays[at].at[:, pl.ds(low, cols)], weights.at[i], arrived.at[sides, i]
        )

    def features_of(side, i):
        return pltpu.make_async_copy(
            tokens[side].at[:, pl.ds(i * depth, depth)], features.at[side, i], arrived.at[side, i]
        )

    def start_all(which):
        for i in range(count):
            rows_of(which, i).start()
            for side in range(sides):
                features_of(side, i).start()

    pl.when(flag[0] == 1)(lambda: start_all(windows[:count]))
    pl.when(flag[0] == 0)(lambda: start_all(windows[count:]))
    for i in range(count):
        rows_of(windows, i).wait()
        for side in range(sides):
            features_of(side, i).wait()
    for side in range(sides):
        for r in range(rows // block):
            here = pl.ds(r * block, block)
            total = jnp.zeros((block, cols), jnp.float32)
            for i in range(count):
                total += jnp.dot(
                    features[side, i, here, :], weights[i], preferred_element_type=jnp.float32
                )
            outs[side][here, :] = total.astype(outs[side].dtype)


def product(is_hub, tokens, cols, at_hub, at_leaf, dtypes):
    (rows, width), depth, sides = tokens[0].shape, at_hub[0][0].shape[0], len(tokens)
    count = len(at_hub)
    arrays, windows = [], []
    for array, low in [*at_hub, *at_leaf]:
        known = [i for i, a in enumerate(arrays) if a is array]
        if not known:
            arrays.append(array)
        windows.append((known[0] if known else len(arrays) - 1, low))
    return pl.pallas_call(
        functools.partial(product_kernel, tuple(windows), count, sides),
        out_shape=[jax.ShapeDtypeStruct((rows, cols), dtype) for dtype in dtypes],
        in_specs=[pl.BlockSpec(memory_space=pltpu.SMEM)]
        + [pl.BlockSpec(memory_space=pl.ANY)] * (sides + len(arrays)),
        out_specs=[pl.BlockSpec(memory_space=pltpu.VMEM)] * sides,
        scratch_shapes=[
            pltpu.VMEM((sides, count, rows, depth), jnp.bfloat16),
            pltpu.VMEM((count, depth, cols), jnp.bfloat16),
            pltpu.SemaphoreType.DMA((sides + 1, count)),
        ],
        compiler_params=pltpu.CompilerParams(vmem_limit_bytes=20 << 20),
        cost_estimate=pl.CostEstimate(flops=0, bytes_accessed=0, transcendentals=0),
        name="product",
    )(is_hub.astype(jnp.int32)[None], *tokens, *arrays)


def kv_columns(kv_weight, head, n_head):
    if n_head == KVH:
        halves = kv_weight[:, :HD], kv_weight[:, HD:]
        has_keys = head < n_head // 2
        first = lax.ppermute(
            jnp.where(has_keys, *halves), "head",
            [(a, 2 * a) if 2 * a < n_head else (a, 2 * a - n_head + 1) for a in range(n_head)],
        )
        second = lax.ppermute(
            jnp.where(has_keys, *halves[::-1]), "head",
            [(a, 2 * a + 1) if 2 * a < n_head else (a, 2 * a - n_head) for a in range(n_head)],
        )
        even = head % 2 == 0
        return [jnp.where(even, first, second), jnp.where(even, second, first)]
    kv_all = lax.all_gather(kv_weight, "head", axis=1, tiled=True)
    kv_head = head * KVH // n_head
    return [
        lax.dynamic_slice_in_dim(kv_all, (part * KVH + kv_head) * HD, HD, 1) for part in range(2)
    ]


def after(value, *others):
    return lax.optimization_barrier((value, *others))[0]


def split_shares(heads, shares):
    total, bounds, sofar = sum(shares), [], 0
    for share in shares:
        bounds.append((sofar * heads // total * HD, (sofar + share) * heads // total * HD))
        sofar += share
    return bounds


def shards(tokens, q_weight, kv_weight, q_gain, k_gain, doc_lengths):
    rows, depth = tokens.shape[0], q_weight.shape[0]
    heads = q_weight.shape[1] // HD
    n_dp, n_head = lax.axis_size("dp"), lax.axis_size("head")
    n_line = n_dp // 2
    n_pairs = n_line // 2
    rank, head = lax.axis_index("dp"), lax.axis_index("head")
    spot, side = rank // 2, rank % 2
    pair = spot // 2

    hub_of = lambda g: 2 * g + 1 if 2 * g < n_pairs else 2 * g
    is_hub = spot % 2 == jnp.where(2 * pair < n_pairs, 1, 0)

    def on_line(moves):
        return [(2 * a + s, 2 * b + s) for a, b in moves for s in range(2)]

    swap = on_line([(a, a ^ 1) for a in range(n_line)])
    outward = on_line([(hub_of(g), hub_of(g) ^ 1) for g in range(n_pairs)])
    across = [(a, a ^ 1) for a in range(n_dp)]
    send = lambda value, moves: lax.ppermute(value, "dp", moves)

    def round_hubs(part):
        return [
            send(part, on_line([(hub_of(g), hub_of((g + s) % n_pairs)) for g in range(n_pairs)]))
            for s in range(1, n_pairs)
        ]

    def to_leaf(parts):
        return [send(part, outward) for part in parts]

    def woven(own, partners, hubs, leaves):
        return [own, partners] + [p for two in zip(hubs, leaves, strict=True) for p in two]

    order = [spot, spot ^ 1]
    for s in range(1, n_pairs):
        source = (pair - s + n_pairs) % n_pairs
        hub = 2 * source + jnp.where(2 * source < n_pairs, 1, 0)
        order += [hub, hub ^ 1]

    def features(block, of_side):
        return jnp.concatenate(
            [lax.dynamic_slice_in_dim(block, (2 * at + of_side) * depth, depth, 1) for at in order],
            axis=1,
        )

    def tables(of_rank):
        lengths = lax.dynamic_index_in_dim(doc_lengths, of_rank, 0, keepdims=False)
        starts = doc_starts(lengths, rows)
        return rope_tables(jnp.arange(rows, dtype=jnp.int32) - starts, starts)

    even = head % 2 == 0
    own_first = q_weight[:, : split_shares(heads, RUNS)[0][1]]
    first = send(own_first, swap)
    twins = [(a, a ^ 1) for a in range(n_head)]
    share = rows // 2
    part = lax.dynamic_slice_in_dim(tokens, head % 2 * share, share, 0)
    part = send(features(after(part, first), 1 - side), across)
    twin = lax.ppermute(part, "head", twins)
    beside_tokens = jnp.concatenate(
        [jnp.where(even, part, twin), jnp.where(even, twin, part)], axis=0
    )
    own_tokens = features(tokens, side)
    own_tables = tables(rank)

    bounds = [b for b in split_shares(heads, RUNS) if b[0] < b[1]]
    count = len(bounds)
    widths = [high - low for low, high in bounds]
    with_kv = 1
    wides = [w + (2 * HD if k == with_kv else 0) for k, w in enumerate(widths)]
    owns = [own_first]
    kv_cols = kv_columns(after(kv_weight, owns[0]), head, n_head)
    owns.append(q_weight[:, bounds[1][0] : bounds[1][1]])
    late_weight = after(q_weight, first)
    owns += [late_weight[:, low:high] for low, high in bounds[2:]]
    owns[with_kv] = jnp.concatenate([owns[with_kv], *kv_cols], axis=1)
    cut = lambda k, where: where[0][:, where[1] : where[1] + wides[k]]
    joined = lambda blocks: jnp.concatenate(blocks, axis=1) if len(blocks) > 1 else blocks[0]

    got, hub_at, leaf_at = {}, {}, {}

    def go_round(own_runs, leaf_run, *ties):
        runs = [(hub_at, k, (owns[k], 0)) for k in own_runs if k < count]
        if leaf_run is not None and leaf_run < count:
            runs.append((leaf_at, leaf_run, got[leaf_run]))
        if runs:
            moved = round_hubs(after(joined([cut(k, where) for _, k, where in runs]), *ties))
            low = 0
            for table, k, _ in runs:
                table[k] = [(p, low) for p in moved]
                low += wides[k]

    got[0] = (first, 0)
    go_round([0], None)
    arrived = lambda table, k: [p for p, _ in table.get(k, [])]
    second = send(joined([after(owns[1], first, *arrived(hub_at, 0))] + owns[2:4]), swap)
    for k in range(1, min(4, count)):
        got[k] = (second, sum(wides[1:k]))
    go_round([], 0)
    go_round([1, 2], None, *arrived(leaf_at, 0))
    go_round([], 1)
    go_round([3], 2, *arrived(leaf_at, 1))

    exchanged, sums, parts, computed = [first, second], [], [], []
    keys = None
    for k in range(count):
        blocks = [owns[k + 4]] if k + 4 < count else []
        low = wides[k + 4] if blocks else 0
        blocks += [cut(k, w) for h, l in zip(hub_at[k], leaf_at[k], strict=True) for w in (h, l)]
        ties = exchanged[-1:] + computed[: max(0, k - 1)][-1:]
        passed = send(after(joined(blocks), *ties), swap)
        exchanged.append(passed)
        if k + 4 < count:
            got[k + 4] = (passed, 0)
        go_round([k + 4], k + 3, *arrived(leaf_at, k + 2))
        wide = wides[k]
        at_leaf = [own_at for own_at in [(owns[k], 0), got[k]]]
        at_leaf += [(passed, low + i * wide) for i in range(2 * (n_pairs - 1))]
        pieces = woven((owns[k], 0), got[k], hub_at[k], leaf_at[k]), at_leaf
        done = parts[: max(0, k - 2 + (k + 1 == count))][-2:]
        theirs, mine = product(
            is_hub, (after(beside_tokens, *computed[-1:], *done), own_tokens), wide, *pieces,
            (jnp.float32 if k == with_kv else jnp.bfloat16, jnp.float32),
        )
        if k == with_kv:
            other_kv = send(theirs[:, widths[k] :], across)
            theirs = theirs[:, : widths[k]].astype(jnp.bfloat16)
        other = send(theirs, across)
        if k == with_kv:
            kv = mine[:, widths[k] :] + other_kv
            mine = mine[:, : widths[k]]
            keys = norm_rope(
                kv[:, :HD], k_gain, own_tables[:, :HD], own_tables[:, HD : 2 * HD],
                lambda n: jnp.concatenate([n[:, HD // 2 :], n[:, : HD // 2]], axis=1),
            )
            keys_values = jnp.concatenate([keys, kv[:, HD:].astype(jnp.bfloat16)], axis=1)
        sums.append((mine, other))
        computed.append(mine)
        if keys is not None:
            late = 1
            while len(parts) < len(sums) - late:
                parts.append(
                    attend(*sums[len(parts)], keys_values, own_tables, q_gain[None, :])
                )
    parts.append(attend(*sums[-1], keys_values, own_tables, q_gain[None, :]))
    return jnp.concatenate(parts, axis=1)


def solution(mesh):
    placed = (P("dp", None), P("dp", "head"), P("dp", "head"), P(), P(), P())
    return jax.shard_map(
        shards, mesh=mesh, in_specs=placed, out_specs=P("dp", "head"), check_vma=False
    )
```

```python
import functools
import math

import jax
import jax.numpy as jnp
from jax import lax
from jax.experimental import pallas as pl
from jax.experimental.pallas import tpu as pltpu
from jax.sharding import PartitionSpec as P

KVH = 4
HD = 128


theta_base = 1000000.0
norm_eps = 1e-06

RUNS = (4, 3, 4, 4, 1)


def doc_starts(lengths, count):
    doc_ends = jnp.cumsum(lengths)
    places = jnp.arange(count, dtype=jnp.int32)
    passed = (places[:, None] >= doc_ends[None, :]).astype(jnp.int32)
    return jnp.sum(passed * lengths[None, :], axis=1)


def rope_tables(positions, starts):
    half_width = HD // 2
    frequency = jnp.exp(
        jnp.arange(half_width, dtype=jnp.float32) * (-2.0 * math.log(theta_base) / HD)
    )
    angles = positions.astype(jnp.float32)[:, None] * frequency[None, :]
    cosine, sine = jnp.cos(angles), jnp.sin(angles)
    wide_starts = jnp.broadcast_to(starts.astype(jnp.float32)[:, None], (starts.shape[0], HD))
    return jnp.concatenate([cosine, cosine, -sine, sine, wide_starts], axis=1)


def norm_rope(raw, gain, cosine, sine, swap_halves):
    inv_rms = lax.rsqrt(jnp.mean(raw * raw, axis=-1, keepdims=True) + norm_eps)
    normed = raw * inv_rms * gain
    return (normed * cosine + swap_halves(normed) * sine).astype(jnp.bfloat16)


def attend_kernel(block, mine, other, keys_values, tables, gain, out):
    rows, cols = mine.shape
    heads = [slice(low, low + HD) for low in range(0, cols, HD)]
    keys, values = keys_values.at[:, :HD], keys_values.at[:, HD:]
    queries = [
        norm_rope(
            mine[:, at] + other[:, at].astype(jnp.float32), gain[...], tables[:, :HD],
            tables[:, HD : 2 * HD], lambda n: pltpu.roll(n, HD // 2, 1),
        )
        for at in heads
    ]
    for first in range(0, rows, block):
        here, upto = slice(first, first + block), first + block
        col = lax.broadcasted_iota(jnp.int32, (block, upto), 1)
        row = lax.broadcasted_iota(jnp.int32, (block, upto), 0) + first
        starts = tables[here, 2 * HD : 2 * HD + 1].astype(jnp.int32)
        allowed = (col >= starts) & (col <= row)
        scores = [
            lax.dot_general(
                q[here], keys[:upto, :], (((1,), (1,)), ((), ())),
                preferred_element_type=jnp.float32,
            )
            for q in queries
        ]
        weights = [
            jnp.where(allowed, jnp.exp2(s * (HD**-0.5 * math.log2(math.e))), 0.0) for s in scores
        ]
        probs = [
            (w * (1.0 / jnp.sum(w, axis=-1, keepdims=True))).astype(jnp.bfloat16) for w in weights
        ]
        for at, p in zip(heads, probs, strict=True):
            mixed = jnp.dot(p, values[:upto, :], preferred_element_type=jnp.float32)
            out[here, at] = mixed.astype(out.dtype)


def attend(mine, other, keys_values, tables, gain):
    rows, cols = mine.shape
    block = 128 if rows % 128 == 0 else rows
    heads = cols // HD
    step = max(n for n in range(1, 5) if heads % n == 0) * HD
    by_heads = pl.BlockSpec((rows, step), lambda h: (0, h))
    whole = lambda a: pl.BlockSpec(a.shape, lambda h: (0, 0))
    return pl.pallas_call(
        functools.partial(attend_kernel, block),
        grid=(cols // step,),
        out_shape=jax.ShapeDtypeStruct((rows, cols), jnp.bfloat16),
        in_specs=[by_heads, by_heads] + [whole(a) for a in (keys_values, tables, gain)],
        out_specs=by_heads,
        compiler_params=pltpu.CompilerParams(vmem_limit_bytes=24 << 20),
        cost_estimate=pl.CostEstimate(flops=0, bytes_accessed=0, transcendentals=0),
        name="attend",
    )(mine, other, keys_values, tables, gain)


def product_kernel(windows, count, sides, flag, *refs):
    tokens, arrays, outs = refs[:sides], refs[sides : -sides - 3], refs[-sides - 3 : -3]
    features, weights, arrived = refs[-3:]
    depth, cols = weights.shape[1:]
    rows = tokens[0].shape[0]
    block = 256 if rows % 256 == 0 else rows

    def rows_of(which, i):
        at, low = which[i]
        return pltpu.make_async_copy(
            arrays[at].at[:, pl.ds(low, cols)], weights.at[i], arrived.at[sides, i]
        )

    def features_of(side, i):
        return pltpu.make_async_copy(
            tokens[side].at[:, pl.ds(i * depth, depth)], features.at[side, i], arrived.at[side, i]
        )

    def start_all(which):
        for i in range(count):
            rows_of(which, i).start()
            for side in range(sides):
                features_of(side, i).start()

    pl.when(flag[0] == 1)(lambda: start_all(windows[:count]))
    pl.when(flag[0] == 0)(lambda: start_all(windows[count:]))
    for side in range(sides):
        for r in range(0, rows, block):
            here = pl.ds(r, block)
            total = jnp.zeros((block, cols), jnp.float32)
            for i in range(count):
                if r == 0:
                    features_of(side, i).wait()
                    if side == 0:
                        rows_of(windows, i).wait()
                total += jnp.dot(
                    features[side, i, here, :], weights[i], preferred_element_type=jnp.float32
                )
            outs[side][here, :] = total.astype(outs[side].dtype)


def product(is_hub, tokens, cols, at_hub, at_leaf, dtypes):
    (rows, width), depth, sides = tokens[0].shape, at_hub[0][0].shape[0], len(tokens)
    count = len(at_hub)
    arrays, windows = [], []
    for array, low in [*at_hub, *at_leaf]:
        known = [i for i, a in enumerate(arrays) if a is array]
        if not known:
            arrays.append(array)
        windows.append((known[0] if known else len(arrays) - 1, low))
    return pl.pallas_call(
        functools.partial(product_kernel, tuple(windows), count, sides),
        out_shape=[jax.ShapeDtypeStruct((rows, cols), dtype) for dtype in dtypes],
        in_specs=[pl.BlockSpec(memory_space=pltpu.SMEM)]
        + [pl.BlockSpec(memory_space=pl.ANY)] * (sides + len(arrays)),
        out_specs=[pl.BlockSpec(memory_space=pltpu.VMEM)] * sides,
        scratch_shapes=[
            pltpu.VMEM((sides, count, rows, depth), jnp.bfloat16),
            pltpu.VMEM((count, depth, cols), jnp.bfloat16),
            pltpu.SemaphoreType.DMA((sides + 1, count)),
        ],
        compiler_params=pltpu.CompilerParams(vmem_limit_bytes=20 << 20),
        cost_estimate=pl.CostEstimate(flops=0, bytes_accessed=0, transcendentals=0),
        name="product",
    )(is_hub.astype(jnp.int32)[None], *tokens, *arrays)


def kv_columns(kv_weight, head, n_head):
    if n_head == KVH:
        halves = kv_weight[:, :HD], kv_weight[:, HD:]
        has_keys = head < n_head // 2
        first = lax.ppermute(
            jnp.where(has_keys, *halves), "head",
            [(a, 2 * a) if 2 * a < n_head else (a, 2 * a - n_head + 1) for a in range(n_head)],
        )
        second = lax.ppermute(
            jnp.where(has_keys, *halves[::-1]), "head",
            [(a, 2 * a + 1) if 2 * a < n_head else (a, 2 * a - n_head) for a in range(n_head)],
        )
        even = head % 2 == 0
        return [jnp.where(even, first, second), jnp.where(even, second, first)]
    kv_all = lax.all_gather(kv_weight, "head", axis=1, tiled=True)
    kv_head = head * KVH // n_head
    return [
        lax.dynamic_slice_in_dim(kv_all, (part * KVH + kv_head) * HD, HD, 1) for part in range(2)
    ]


def after(value, *others):
    return lax.optimization_barrier((value, *others))[0]


def split_shares(heads, shares):
    total, bounds, sofar = sum(shares), [], 0
    for share in shares:
        bounds.append((sofar * heads // total * HD, (sofar + share) * heads // total * HD))
        sofar += share
    return bounds


def shards(tokens, q_weight, kv_weight, q_gain, k_gain, doc_lengths):
    rows, depth = tokens.shape[0], q_weight.shape[0]
    heads = q_weight.shape[1] // HD
    n_dp, n_head = lax.axis_size("dp"), lax.axis_size("head")
    n_line = n_dp // 2
    n_pairs = n_line // 2
    rank, head = lax.axis_index("dp"), lax.axis_index("head")
    spot, side = rank // 2, rank % 2
    pair = spot // 2

    hub_of = lambda g: 2 * g + 1 if 2 * g < n_pairs else 2 * g
    is_hub = spot % 2 == jnp.where(2 * pair < n_pairs, 1, 0)

    def on_line(moves):
        return [(2 * a + s, 2 * b + s) for a, b in moves for s in range(2)]

    swap = on_line([(a, a ^ 1) for a in range(n_line)])
    outward = on_line([(hub_of(g), hub_of(g) ^ 1) for g in range(n_pairs)])
    across = [(a, a ^ 1) for a in range(n_dp)]
    send = lambda value, moves: lax.ppermute(value, "dp", moves)

    def round_hubs(part):
        return [
            send(part, on_line([(hub_of(g), hub_of((g + s) % n_pairs)) for g in range(n_pairs)]))
            for s in range(1, n_pairs)
        ]

    def to_leaf(parts):
        return [send(part, outward) for part in parts]

    def woven(own, partners, hubs, leaves):
        return [own, partners] + [p for two in zip(hubs, leaves, strict=True) for p in two]

    order = [spot, spot ^ 1]
    for s in range(1, n_pairs):
        source = (pair - s + n_pairs) % n_pairs
        hub = 2 * source + jnp.where(2 * source < n_pairs, 1, 0)
        order += [hub, hub ^ 1]

    def features(block, of_side):
        return jnp.concatenate(
            [lax.dynamic_slice_in_dim(block, (2 * at + of_side) * depth, depth, 1) for at in order],
            axis=1,
        )

    def tables(of_rank):
        lengths = lax.dynamic_index_in_dim(doc_lengths, of_rank, 0, keepdims=False)
        starts = doc_starts(lengths, rows)
        return rope_tables(jnp.arange(rows, dtype=jnp.int32) - starts, starts)

    even = head % 2 == 0
    own_first = q_weight[:, : split_shares(heads, RUNS)[0][1]]
    first = send(own_first, swap)
    twins = [(a, a ^ 1) for a in range(n_head)]
    share = rows // 2
    part = lax.dynamic_slice_in_dim(tokens, head % 2 * share, share, 0)
    part = send(features(part, 1 - side), across)
    twin = lax.ppermute(part, "head", twins)
    beside_tokens = jnp.concatenate(
        [jnp.where(even, part, twin), jnp.where(even, twin, part)], axis=0
    )
    own_tokens = features(tokens, side)
    own_tables = tables(rank)

    bounds = [b for b in split_shares(heads, RUNS) if b[0] < b[1]]
    count = len(bounds)
    widths = [high - low for low, high in bounds]
    with_kv = 1
    wides = [w + (2 * HD if k == with_kv else 0) for k, w in enumerate(widths)]
    owns = [own_first]
    kv_cols = kv_columns(after(kv_weight, owns[0]), head, n_head)
    owns.append(q_weight[:, bounds[1][0] : bounds[1][1]])
    late_weight = after(q_weight, first)
    owns += [late_weight[:, low:high] for low, high in bounds[2:]]
    owns[with_kv] = jnp.concatenate([owns[with_kv], *kv_cols], axis=1)
    cut = lambda k, where: where[0][:, where[1] : where[1] + wides[k]]
    joined = lambda blocks: jnp.concatenate(blocks, axis=1) if len(blocks) > 1 else blocks[0]

    got, hub_at, leaf_at = {}, {}, {}

    def go_round(own_runs, leaf_run, *ties):
        runs = [(hub_at, k, (owns[k], 0)) for k in own_runs if k < count]
        if leaf_run is not None and leaf_run < count:
            runs.append((leaf_at, leaf_run, got[leaf_run]))
        if runs:
            moved = round_hubs(after(joined([cut(k, where) for _, k, where in runs]), *ties))
            low = 0
            for table, k, _ in runs:
                table[k] = [(p, low) for p in moved]
                low += wides[k]

    got[0] = (first, 0)
    go_round([0], None)
    arrived = lambda table, k: [p for p, _ in table.get(k, [])]
    second = send(joined(owns[1:4]), swap)
    for k in range(1, min(4, count)):
        got[k] = (second, sum(wides[1:k]))
    go_round([], 0)
    go_round([1, 2], None, *arrived(leaf_at, 0))
    go_round([], 1)
    go_round([3], 2, *arrived(leaf_at, 1))

    exchanged, sums, parts, computed = [first, second], [], [], []
    keys = None
    for k in range(count):
        blocks = [owns[k + 4]] if k + 4 < count else []
        low = wides[k + 4] if blocks else 0
        blocks += [cut(k, w) for h, l in zip(hub_at[k], leaf_at[k], strict=True) for w in (h, l)]
        ties = exchanged[-1:] + computed[: max(0, k - 1)][-1:]
        passed = send(after(joined(blocks), *ties), swap)
        exchanged.append(passed)
        if k + 4 < count:
            got[k + 4] = (passed, 0)
        go_round([k + 4], k + 3, *arrived(leaf_at, k + 2))
        wide = wides[k]
        at_leaf = [(owns[k], 0), got[k]]
        at_leaf += [(passed, low + i * wide) for i in range(2 * (n_pairs - 1))]
        pieces = woven((owns[k], 0), got[k], hub_at[k], leaf_at[k]), at_leaf
        done = parts[: max(0, k - 2 + (k + 1 == count))][-2:]
        theirs, mine = product(
            is_hub, (after(beside_tokens, *computed[-1:], *done), own_tokens), wide, *pieces,
            (jnp.float32 if k == with_kv else jnp.bfloat16, jnp.float32),
        )
        if k == with_kv:
            other_kv = send(theirs[:, widths[k] :], across)
            theirs = theirs[:, : widths[k]].astype(jnp.bfloat16)
        other = send(theirs, across)
        if k == with_kv:
            kv = mine[:, widths[k] :] + other_kv
            mine = mine[:, : widths[k]]
            keys = norm_rope(
                kv[:, :HD], k_gain, own_tables[:, :HD], own_tables[:, HD : 2 * HD],
                lambda n: jnp.concatenate([n[:, HD // 2 :], n[:, : HD // 2]], axis=1),
            )
            keys_values = jnp.concatenate([keys, kv[:, HD:].astype(jnp.bfloat16)], axis=1)
        sums.append((mine, other))
        computed.append(mine)
        if keys is not None:
            while len(parts) < len(sums) - 1:
                parts.append(
                    attend(*sums[len(parts)], keys_values, own_tables, q_gain[None, :])
                )
    last, other = sums[-1]
    parts.append(attend(after(last, *parts[-1:]), other, keys_values, own_tables, q_gain[None, :]))
    return jnp.concatenate(parts, axis=1)


def solution(mesh):
    placed = (P("dp", None), P("dp", "head"), P("dp", "head"), P(), P(), P())
    return jax.shard_map(
        shards, mesh=mesh, in_specs=placed, out_specs=P("dp", "head"), check_vma=False
    )
```

```python
import functools
import math

import jax
import jax.numpy as jnp
from jax import lax
from jax.experimental import pallas as pl
from jax.experimental.pallas import tpu as pltpu
from jax.sharding import PartitionSpec as P

KVH = 4
HD = 128


theta_base = 1000000.0
norm_eps = 1e-06

RUNS = (4, 3, 4, 4, 1)


def doc_starts(lengths, count):
    doc_ends = jnp.cumsum(lengths)
    places = jnp.arange(count, dtype=jnp.int32)
    passed = (places[:, None] >= doc_ends[None, :]).astype(jnp.int32)
    return jnp.sum(passed * lengths[None, :], axis=1)


def rope_tables(positions, starts):
    half_width = HD // 2
    frequency = jnp.exp(
        jnp.arange(half_width, dtype=jnp.float32) * (-2.0 * math.log(theta_base) / HD)
    )
    angles = positions.astype(jnp.float32)[:, None] * frequency[None, :]
    cosine, sine = jnp.cos(angles), jnp.sin(angles)
    wide_starts = jnp.broadcast_to(starts.astype(jnp.float32)[:, None], (starts.shape[0], HD))
    return jnp.concatenate([cosine, cosine, -sine, sine, wide_starts], axis=1)


def norm_rope(raw, gain, cosine, sine, swap_halves):
    inv_rms = lax.rsqrt(jnp.mean(raw * raw, axis=-1, keepdims=True) + norm_eps)
    normed = raw * inv_rms * gain
    return (normed * cosine + swap_halves(normed) * sine).astype(jnp.bfloat16)


def attend_kernel(block, mine, other, keys_values, tables, gain, out):
    rows, cols = mine.shape
    heads = [slice(low, low + HD) for low in range(0, cols, HD)]
    keys, values = keys_values.at[:, :HD], keys_values.at[:, HD:]
    queries = [
        norm_rope(
            mine[:, at] + other[:, at].astype(jnp.float32), gain[...], tables[:, :HD],
            tables[:, HD : 2 * HD], lambda n: pltpu.roll(n, HD // 2, 1),
        )
        for at in heads
    ]
    for first in range(0, rows, block):
        here, upto = slice(first, first + block), first + block
        col = lax.broadcasted_iota(jnp.int32, (block, upto), 1)
        row = lax.broadcasted_iota(jnp.int32, (block, upto), 0) + first
        starts = tables[here, 2 * HD : 2 * HD + 1].astype(jnp.int32)
        allowed = (col >= starts) & (col <= row)
        scores = [
            lax.dot_general(
                q[here], keys[:upto, :], (((1,), (1,)), ((), ())),
                preferred_element_type=jnp.float32,
            )
            for q in queries
        ]
        weights = [
            jnp.where(allowed, jnp.exp2(s * (HD**-0.5 * math.log2(math.e))), 0.0) for s in scores
        ]
        probs = [
            (w * (1.0 / jnp.sum(w, axis=-1, keepdims=True))).astype(jnp.bfloat16) for w in weights
        ]
        for at, p in zip(heads, probs, strict=True):
            mixed = jnp.dot(p, values[:upto, :], preferred_element_type=jnp.float32)
            out[here, at] = mixed.astype(out.dtype)


def attend(mine, other, keys_values, tables, gain):
    rows, cols = mine.shape
    block = 128 if rows % 128 == 0 else rows
    heads = cols // HD
    step = max(n for n in range(1, 5) if heads % n == 0) * HD
    by_heads = pl.BlockSpec((rows, step), lambda h: (0, h))
    whole = lambda a: pl.BlockSpec(a.shape, lambda h: (0, 0))
    return pl.pallas_call(
        functools.partial(attend_kernel, block),
        grid=(cols // step,),
        out_shape=jax.ShapeDtypeStruct((rows, cols), jnp.bfloat16),
        in_specs=[by_heads, by_heads] + [whole(a) for a in (keys_values, tables, gain)],
        out_specs=by_heads,
        compiler_params=pltpu.CompilerParams(vmem_limit_bytes=24 << 20),
        cost_estimate=pl.CostEstimate(flops=0, bytes_accessed=0, transcendentals=0),
        name="attend",
    )(mine, other, keys_values, tables, gain)


def product_kernel(windows, count, sides, flag, *refs):
    tokens, arrays, outs = refs[:sides], refs[sides : -sides - 3], refs[-sides - 3 : -3]
    features, weights, arrived = refs[-3:]
    depth, cols = weights.shape[1:]
    rows = tokens[0].shape[0]
    block = 256 if rows % 256 == 0 else rows

    def rows_of(which, i):
        at, low = which[i]
        return pltpu.make_async_copy(
            arrays[at].at[:, pl.ds(low, cols)], weights.at[i], arrived.at[sides, i]
        )

    def features_of(side, i):
        return pltpu.make_async_copy(
            tokens[side].at[:, pl.ds(i * depth, depth)], features.at[side, i], arrived.at[side, i]
        )

    def start_all(which):
        for i in range(count):
            rows_of(which, i).start()
            for side in range(sides):
                features_of(side, i).start()

    pl.when(flag[0] == 1)(lambda: start_all(windows[:count]))
    pl.when(flag[0] == 0)(lambda: start_all(windows[count:]))
    for side in range(sides):
        for r in range(0, rows, block):
            here = pl.ds(r, block)
            total = jnp.zeros((block, cols), jnp.float32)
            for i in range(count):
                if r == 0:
                    features_of(side, i).wait()
                    if side == 0:
                        rows_of(windows, i).wait()
                total += jnp.dot(
                    features[side, i, here, :], weights[i], preferred_element_type=jnp.float32
                )
            outs[side][here, :] = total.astype(outs[side].dtype)


def product(is_hub, tokens, cols, at_hub, at_leaf, dtypes):
    (rows, width), depth, sides = tokens[0].shape, at_hub[0][0].shape[0], len(tokens)
    count = len(at_hub)
    arrays, windows = [], []
    for array, low in [*at_hub, *at_leaf]:
        known = [i for i, a in enumerate(arrays) if a is array]
        if not known:
            arrays.append(array)
        windows.append((known[0] if known else len(arrays) - 1, low))
    return pl.pallas_call(
        functools.partial(product_kernel, tuple(windows), count, sides),
        out_shape=[jax.ShapeDtypeStruct((rows, cols), dtype) for dtype in dtypes],
        in_specs=[pl.BlockSpec(memory_space=pltpu.SMEM)]
        + [pl.BlockSpec(memory_space=pl.ANY)] * (sides + len(arrays)),
        out_specs=[pl.BlockSpec(memory_space=pltpu.VMEM)] * sides,
        scratch_shapes=[
            pltpu.VMEM((sides, count, rows, depth), jnp.bfloat16),
            pltpu.VMEM((count, depth, cols), jnp.bfloat16),
            pltpu.SemaphoreType.DMA((sides + 1, count)),
        ],
        compiler_params=pltpu.CompilerParams(vmem_limit_bytes=20 << 20),
        cost_estimate=pl.CostEstimate(flops=0, bytes_accessed=0, transcendentals=0),
        name="product",
    )(is_hub.astype(jnp.int32)[None], *tokens, *arrays)


def kv_columns(kv_weight, head, n_head):
    if n_head == KVH:
        halves = kv_weight[:, :HD], kv_weight[:, HD:]
        has_keys = head < n_head // 2
        first = lax.ppermute(
            jnp.where(has_keys, *halves), "head",
            [(a, 2 * a) if 2 * a < n_head else (a, 2 * a - n_head + 1) for a in range(n_head)],
        )
        second = lax.ppermute(
            jnp.where(has_keys, *halves[::-1]), "head",
            [(a, 2 * a + 1) if 2 * a < n_head else (a, 2 * a - n_head) for a in range(n_head)],
        )
        even = head % 2 == 0
        return [jnp.where(even, first, second), jnp.where(even, second, first)]
    kv_all = lax.all_gather(kv_weight, "head", axis=1, tiled=True)
    kv_head = head * KVH // n_head
    return [
        lax.dynamic_slice_in_dim(kv_all, (part * KVH + kv_head) * HD, HD, 1) for part in range(2)
    ]


def after(value, *others):
    return lax.optimization_barrier((value, *others))[0]


def split_shares(heads, shares):
    total, bounds, sofar = sum(shares), [], 0
    for share in shares:
        bounds.append((sofar * heads // total * HD, (sofar + share) * heads // total * HD))
        sofar += share
    return bounds


def shards(tokens, q_weight, kv_weight, q_gain, k_gain, doc_lengths):
    rows, depth = tokens.shape[0], q_weight.shape[0]
    heads = q_weight.shape[1] // HD
    n_dp, n_head = lax.axis_size("dp"), lax.axis_size("head")
    n_line = n_dp // 2
    n_pairs = n_line // 2
    rank, head = lax.axis_index("dp"), lax.axis_index("head")
    spot, side = rank // 2, rank % 2
    pair = spot // 2

    hub_of = lambda g: 2 * g + 1 if 2 * g < n_pairs else 2 * g
    is_hub = spot % 2 == jnp.where(2 * pair < n_pairs, 1, 0)

    def on_line(moves):
        return [(2 * a + s, 2 * b + s) for a, b in moves for s in range(2)]

    swap = on_line([(a, a ^ 1) for a in range(n_line)])
    outward = on_line([(hub_of(g), hub_of(g) ^ 1) for g in range(n_pairs)])
    across = [(a, a ^ 1) for a in range(n_dp)]
    send = lambda value, moves: lax.ppermute(value, "dp", moves)

    def round_hubs(part):
        return [
            send(part, on_line([(hub_of(g), hub_of((g + s) % n_pairs)) for g in range(n_pairs)]))
            for s in range(1, n_pairs)
        ]

    def to_leaf(parts):
        return [send(part, outward) for part in parts]

    def woven(own, partners, hubs, leaves):
        return [own, partners] + [p for two in zip(hubs, leaves, strict=True) for p in two]

    order = [spot, spot ^ 1]
    for s in range(1, n_pairs):
        source = (pair - s + n_pairs) % n_pairs
        hub = 2 * source + jnp.where(2 * source < n_pairs, 1, 0)
        order += [hub, hub ^ 1]

    def features(block, of_side):
        return jnp.concatenate(
            [lax.dynamic_slice_in_dim(block, (2 * at + of_side) * depth, depth, 1) for at in order],
            axis=1,
        )

    def tables(of_rank):
        lengths = lax.dynamic_index_in_dim(doc_lengths, of_rank, 0, keepdims=False)
        starts = doc_starts(lengths, rows)
        return rope_tables(jnp.arange(rows, dtype=jnp.int32) - starts, starts)

    even = head % 2 == 0
    own_first = q_weight[:, : split_shares(heads, RUNS)[0][1]]
    first = send(own_first, swap)
    twins = [(a, a ^ 1) for a in range(n_head)]
    share = rows // 2
    part = lax.dynamic_slice_in_dim(tokens, head % 2 * share, share, 0)
    part = send(features(after(part), 1 - side), across)
    twin = lax.ppermute(part, "head", twins)
    beside_tokens = jnp.concatenate(
        [jnp.where(even, part, twin), jnp.where(even, twin, part)], axis=0
    )
    own_tokens = features(tokens, side)
    own_tables = tables(rank)

    bounds = [b for b in split_shares(heads, RUNS) if b[0] < b[1]]
    count = len(bounds)
    widths = [high - low for low, high in bounds]
    with_kv = 1
    wides = [w + (2 * HD if k == with_kv else 0) for k, w in enumerate(widths)]
    owns = [own_first]
    kv_cols = kv_columns(after(kv_weight, owns[0]), head, n_head)
    owns.append(q_weight[:, bounds[1][0] : bounds[1][1]])
    late_weight = after(q_weight, first)
    owns += [late_weight[:, low:high] for low, high in bounds[2:]]
    owns[with_kv] = jnp.concatenate([owns[with_kv], *kv_cols], axis=1)
    cut = lambda k, where: where[0][:, where[1] : where[1] + wides[k]]
    joined = lambda blocks: jnp.concatenate(blocks, axis=1) if len(blocks) > 1 else blocks[0]

    got, hub_at, leaf_at = {}, {}, {}

    def go_round(own_runs, leaf_run, *ties):
        runs = [(hub_at, k, (owns[k], 0)) for k in own_runs if k < count]
        if leaf_run is not None and leaf_run < count:
            runs.append((leaf_at, leaf_run, got[leaf_run]))
        if runs:
            moved = round_hubs(after(joined([cut(k, where) for _, k, where in runs]), *ties))
            low = 0
            for table, k, _ in runs:
                table[k] = [(p, low) for p in moved]
                low += wides[k]

    got[0] = (first, 0)
    go_round([0], None)
    arrived = lambda table, k: [p for p, _ in table.get(k, [])]
    second = send(joined([after(owns[1])] + owns[2:4]), swap)
    for k in range(1, min(4, count)):
        got[k] = (second, sum(wides[1:k]))
    go_round([], 0)
    go_round([1, 2], None, *arrived(leaf_at, 0))
    go_round([], 1)
    go_round([3], 2, *arrived(leaf_at, 1))

    exchanged, sums, parts, computed = [first, second], [], [], []
    keys = None
    for k in range(count):
        blocks = [owns[k + 4]] if k + 4 < count else []
        low = wides[k + 4] if blocks else 0
        blocks += [cut(k, w) for h, l in zip(hub_at[k], leaf_at[k], strict=True) for w in (h, l)]
        ties = exchanged[-1:] + computed[: max(0, k - 1)][-1:]
        passed = send(after(joined(blocks), *ties), swap)
        exchanged.append(passed)
        if k + 4 < count:
            got[k + 4] = (passed, 0)
        go_round([k + 4], k + 3, *arrived(leaf_at, k + 2))
        wide = wides[k]
        at_leaf = [(owns[k], 0), got[k]]
        at_leaf += [(passed, low + i * wide) for i in range(2 * (n_pairs - 1))]
        pieces = woven((owns[k], 0), got[k], hub_at[k], leaf_at[k]), at_leaf
        done = parts[: max(0, k - 2 + (k + 1 == count))][-2:]
        theirs, mine = product(
            is_hub, (after(beside_tokens, *computed[-1:], *done), own_tokens), wide, *pieces,
            (jnp.float32 if k == with_kv else jnp.bfloat16, jnp.float32),
        )
        if k == with_kv:
            other_kv = send(theirs[:, widths[k] :], across)
            theirs = theirs[:, : widths[k]].astype(jnp.bfloat16)
        other = send(theirs, across)
        if k == with_kv:
            kv = mine[:, widths[k] :] + other_kv
            mine = mine[:, : widths[k]]
            keys = norm_rope(
                kv[:, :HD], k_gain, own_tables[:, :HD], own_tables[:, HD : 2 * HD],
                lambda n: jnp.concatenate([n[:, HD // 2 :], n[:, : HD // 2]], axis=1),
            )
            keys_values = jnp.concatenate([keys, kv[:, HD:].astype(jnp.bfloat16)], axis=1)
        sums.append((mine, other))
        computed.append(mine)
        if keys is not None:
            while len(parts) < len(sums) - 1:
                parts.append(
                    attend(*sums[len(parts)], keys_values, own_tables, q_gain[None, :])
                )
    last, other = sums[-1]
    parts.append(attend(after(last, *parts[-1:]), other, keys_values, own_tables, q_gain[None, :]))
    return jnp.concatenate(parts, axis=1)


def solution(mesh):
    placed = (P("dp", None), P("dp", "head"), P("dp", "head"), P(), P(), P())
    return jax.shard_map(
        shards, mesh=mesh, in_specs=placed, out_specs=P("dp", "head"), check_vma=False
    )
```

```python
import functools
import math

import jax
import jax.numpy as jnp
from jax import lax
from jax.experimental import pallas as pl
from jax.experimental.pallas import tpu as pltpu
from jax.sharding import PartitionSpec as P

KVH = 4
HD = 128


theta_base = 1000000.0
norm_eps = 1e-06

RUNS = (4, 3, 4, 4, 1)


def doc_starts(lengths, count):
    doc_ends = jnp.cumsum(lengths)
    places = jnp.arange(count, dtype=jnp.int32)
    passed = (places[:, None] >= doc_ends[None, :]).astype(jnp.int32)
    return jnp.sum(passed * lengths[None, :], axis=1)


def rope_tables(positions, starts):
    half_width = HD // 2
    frequency = jnp.exp(
        jnp.arange(half_width, dtype=jnp.float32) * (-2.0 * math.log(theta_base) / HD)
    )
    angles = positions.astype(jnp.float32)[:, None] * frequency[None, :]
    cosine, sine = jnp.cos(angles), jnp.sin(angles)
    wide_starts = jnp.broadcast_to(starts.astype(jnp.float32)[:, None], (starts.shape[0], HD))
    return jnp.concatenate([cosine, cosine, -sine, sine, wide_starts], axis=1)


def norm_rope(raw, gain, cosine, sine, swap_halves):
    inv_rms = lax.rsqrt(jnp.mean(raw * raw, axis=-1, keepdims=True) + norm_eps)
    normed = raw * inv_rms * gain
    return (normed * cosine + swap_halves(normed) * sine).astype(jnp.bfloat16)


def attend_kernel(block, mine, other, keys_values, tables, gain, out):
    rows, cols = mine.shape
    heads = [slice(low, low + HD) for low in range(0, cols, HD)]
    keys, values = keys_values.at[:, :HD], keys_values.at[:, HD:]
    queries = [
        norm_rope(
            mine[:, at] + other[:, at].astype(jnp.float32), gain[...], tables[:, :HD],
            tables[:, HD : 2 * HD], lambda n: pltpu.roll(n, HD // 2, 1),
        )
        for at in heads
    ]
    for first in range(0, rows, block):
        here, upto = slice(first, first + block), first + block
        col = lax.broadcasted_iota(jnp.int32, (block, upto), 1)
        row = lax.broadcasted_iota(jnp.int32, (block, upto), 0) + first
        starts = tables[here, 2 * HD : 2 * HD + 1].astype(jnp.int32)
        allowed = (col >= starts) & (col <= row)
        scores = [
            lax.dot_general(
                q[here], keys[:upto, :], (((1,), (1,)), ((), ())),
                preferred_element_type=jnp.float32,
            )
            for q in queries
        ]
        weights = [
            jnp.where(allowed, jnp.exp2(s * (HD**-0.5 * math.log2(math.e))), 0.0) for s in scores
        ]
        probs = [
            (w * (1.0 / jnp.sum(w, axis=-1, keepdims=True))).astype(jnp.bfloat16) for w in weights
        ]
        for at, p in zip(heads, probs, strict=True):
            mixed = jnp.dot(p, values[:upto, :], preferred_element_type=jnp.float32)
            out[here, at] = mixed.astype(out.dtype)


def attend(mine, other, keys_values, tables, gain):
    rows, cols = mine.shape
    block = 128 if rows % 128 == 0 else rows
    heads = cols // HD
    step = max(n for n in range(1, 5) if heads % n == 0) * HD
    by_heads = pl.BlockSpec((rows, step), lambda h: (0, h))
    whole = lambda a: pl.BlockSpec(a.shape, lambda h: (0, 0))
    return pl.pallas_call(
        functools.partial(attend_kernel, block),
        grid=(cols // step,),
        out_shape=jax.ShapeDtypeStruct((rows, cols), jnp.bfloat16),
        in_specs=[by_heads, by_heads] + [whole(a) for a in (keys_values, tables, gain)],
        out_specs=by_heads,
        compiler_params=pltpu.CompilerParams(vmem_limit_bytes=16 << 20),
        cost_estimate=pl.CostEstimate(flops=0, bytes_accessed=0, transcendentals=0),
        name="attend",
    )(mine, other, keys_values, tables, gain)


def product_kernel(windows, count, sides, base, flag, *refs):
    tokens, arrays, outs = refs[:sides], refs[sides : -sides - 3], refs[-sides - 3 : -3]
    n_arrays = max(at for at, _ in windows) + 1
    arrays, so_far = arrays[:n_arrays], arrays[n_arrays:]
    features, weights, arrived = refs[-3:]
    depth, cols = weights.shape[1:]
    rows = tokens[0].shape[0]
    block = 256 if rows % 256 == 0 else rows

    def rows_of(which, i):
        at, low = which[i]
        return pltpu.make_async_copy(
            arrays[at].at[:, pl.ds(low, cols)], weights.at[i], arrived.at[sides, i]
        )

    def features_of(side, i):
        return pltpu.make_async_copy(
            tokens[side].at[:, pl.ds((base + i) * depth, depth)], features.at[side, i], arrived.at[side, i]
        )

    def start_all(which):
        for i in range(count):
            rows_of(which, i).start()
            for side in range(sides):
                features_of(side, i).start()

    pl.when(flag[0] == 1)(lambda: start_all(windows[:count]))
    pl.when(flag[0] == 0)(lambda: start_all(windows[count:]))
    for side in range(sides):
        for r in range(0, rows, block):
            here = pl.ds(r, block)
            total = so_far[side][here, :] if so_far else jnp.zeros((block, cols), jnp.float32)
            for i in range(count):
                if r == 0:
                    features_of(side, i).wait()
                    if side == 0:
                        rows_of(windows, i).wait()
                total += jnp.dot(
                    features[side, i, here, :], weights[i], preferred_element_type=jnp.float32
                )
            outs[side][here, :] = total.astype(outs[side].dtype)


def product(is_hub, tokens, cols, at_hub, at_leaf, dtypes, base=0, so_far=()):
    (rows, width), depth, sides = tokens[0].shape, at_hub[0][0].shape[0], len(tokens)
    count = len(at_hub)
    arrays, windows = [], []
    for array, low in [*at_hub, *at_leaf]:
        known = [i for i, a in enumerate(arrays) if a is array]
        if not known:
            arrays.append(array)
        windows.append((known[0] if known else len(arrays) - 1, low))
    return pl.pallas_call(
        functools.partial(product_kernel, tuple(windows), count, sides, base),
        out_shape=[jax.ShapeDtypeStruct((rows, cols), dtype) for dtype in dtypes],
        in_specs=[pl.BlockSpec(memory_space=pltpu.SMEM)]
        + [pl.BlockSpec(memory_space=pl.ANY)] * (sides + len(arrays))
        + [pl.BlockSpec(memory_space=pltpu.VMEM)] * len(so_far),
        out_specs=[pl.BlockSpec(memory_space=pltpu.VMEM)] * sides,
        scratch_shapes=[
            pltpu.VMEM((sides, count, rows, depth), jnp.bfloat16),
            pltpu.VMEM((count, depth, cols), jnp.bfloat16),
            pltpu.SemaphoreType.DMA((sides + 1, count)),
        ],
        compiler_params=pltpu.CompilerParams(vmem_limit_bytes=16 << 20),
        cost_estimate=pl.CostEstimate(flops=2 * rows * cols * width, bytes_accessed=0, transcendentals=0),
        name="product",
    )(is_hub.astype(jnp.int32)[None], *tokens, *arrays, *so_far)


def kv_columns(kv_weight, head, n_head):
    if n_head == KVH:
        halves = kv_weight[:, :HD], kv_weight[:, HD:]
        has_keys = head < n_head // 2
        first = lax.ppermute(
            jnp.where(has_keys, *halves), "head",
            [(a, 2 * a) if 2 * a < n_head else (a, 2 * a - n_head + 1) for a in range(n_head)],
        )
        second = lax.ppermute(
            jnp.where(has_keys, *halves[::-1]), "head",
            [(a, 2 * a + 1) if 2 * a < n_head else (a, 2 * a - n_head) for a in range(n_head)],
        )
        even = head % 2 == 0
        return [jnp.where(even, first, second), jnp.where(even, second, first)]
    kv_all = lax.all_gather(kv_weight, "head", axis=1, tiled=True)
    kv_head = head * KVH // n_head
    return [
        lax.dynamic_slice_in_dim(kv_all, (part * KVH + kv_head) * HD, HD, 1) for part in range(2)
    ]


def after(value, *others):
    return lax.optimization_barrier((value, *others))[0]


def split_shares(heads, shares):
    total, bounds, sofar = sum(shares), [], 0
    for share in shares:
        bounds.append((sofar * heads // total * HD, (sofar + share) * heads // total * HD))
        sofar += share
    return bounds


def shards(tokens, q_weight, kv_weight, q_gain, k_gain, doc_lengths):
    rows, depth = tokens.shape[0], q_weight.shape[0]
    heads = q_weight.shape[1] // HD
    n_dp, n_head = lax.axis_size("dp"), lax.axis_size("head")
    n_line = n_dp // 2
    n_pairs = n_line // 2
    rank, head = lax.axis_index("dp"), lax.axis_index("head")
    spot, side = rank // 2, rank % 2
    pair = spot // 2

    hub_of = lambda g: 2 * g + 1 if 2 * g < n_pairs else 2 * g
    is_hub = spot % 2 == jnp.where(2 * pair < n_pairs, 1, 0)

    def on_line(moves):
        return [(2 * a + s, 2 * b + s) for a, b in moves for s in range(2)]

    swap = on_line([(a, a ^ 1) for a in range(n_line)])
    across = [(a, a ^ 1) for a in range(n_dp)]
    send = lambda value, moves: lax.ppermute(value, "dp", moves)

    def round_hubs(part):
        return [
            send(part, on_line([(hub_of(g), hub_of((g + s) % n_pairs)) for g in range(n_pairs)]))
            for s in range(1, n_pairs)
        ]

    def woven(own, partners, hubs, leaves):
        return [own, partners] + [p for two in zip(hubs, leaves, strict=True) for p in two]

    order = [spot, spot ^ 1]
    for s in range(1, n_pairs):
        source = (pair - s + n_pairs) % n_pairs
        hub = 2 * source + jnp.where(2 * source < n_pairs, 1, 0)
        order += [hub, hub ^ 1]

    def features(block, of_side):
        return jnp.concatenate(
            [lax.dynamic_slice_in_dim(block, (2 * at + of_side) * depth, depth, 1) for at in order],
            axis=1,
        )

    def tables(of_rank):
        lengths = lax.dynamic_index_in_dim(doc_lengths, of_rank, 0, keepdims=False)
        starts = doc_starts(lengths, rows)
        return rope_tables(jnp.arange(rows, dtype=jnp.int32) - starts, starts)

    even = head % 2 == 0
    own_first = q_weight[:, : split_shares(heads, RUNS)[0][1]]
    first = send(own_first, swap)
    twins = [(a, a ^ 1) for a in range(n_head)]
    share = rows // 2
    part = lax.dynamic_slice_in_dim(tokens, head % 2 * share, share, 0)
    part = send(features(after(part), 1 - side), across)
    twin = lax.ppermute(part, "head", twins)
    beside_tokens = jnp.concatenate(
        [jnp.where(even, part, twin), jnp.where(even, twin, part)], axis=0
    )
    own_tokens = features(tokens, side)
    own_tables = tables(rank)

    bounds = [b for b in split_shares(heads, RUNS) if b[0] < b[1]]
    count = len(bounds)
    widths = [high - low for low, high in bounds]
    with_kv = 1
    wides = [w + (2 * HD if k == with_kv else 0) for k, w in enumerate(widths)]
    owns = [own_first]
    kv_cols = kv_columns(after(kv_weight, owns[0]), head, n_head)
    owns.append(q_weight[:, bounds[1][0] : bounds[1][1]])
    late_weight = after(q_weight, first)
    owns += [late_weight[:, low:high] for low, high in bounds[2:]]
    owns[with_kv] = jnp.concatenate([owns[with_kv], *kv_cols], axis=1)
    cut = lambda k, where: where[0][:, where[1] : where[1] + wides[k]]
    joined = lambda blocks: jnp.concatenate(blocks, axis=1) if len(blocks) > 1 else blocks[0]

    got, hub_at, leaf_at = {}, {}, {}

    def go_round(own_runs, leaf_run, *ties):
        runs = [(hub_at, k, (owns[k], 0)) for k in own_runs if k < count]
        if leaf_run is not None and leaf_run < count:
            runs.append((leaf_at, leaf_run, got[leaf_run]))
        if runs:
            moved = round_hubs(after(joined([cut(k, where) for _, k, where in runs]), *ties))
            low = 0
            for table, k, _ in runs:
                table[k] = [(p, low) for p in moved]
                low += wides[k]

    got[0] = (first, 0)
    go_round([0], None)
    arrived = lambda table, k: [p for p, _ in table.get(k, [])]
    second = send(joined([after(owns[1])] + owns[2:4]), swap)
    for k in range(1, min(4, count)):
        got[k] = (second, sum(wides[1:k]))
    go_round([], 0)
    go_round([1, 2], None, *arrived(leaf_at, 0))
    go_round([], 1)
    go_round([3], 2, *arrived(leaf_at, 1))

    exchanged, sums, parts, computed = [first, second], [], [], []
    keys = None
    for k in range(count):
        blocks = [owns[k + 4]] if k + 4 < count else []
        low = wides[k + 4] if blocks else 0
        blocks += [cut(k, w) for h, l in zip(hub_at[k], leaf_at[k], strict=True) for w in (h, l)]
        ties = exchanged[-1:] + computed[: max(0, k - 1)][-1:]
        passed = send(after(joined(blocks), *ties), swap)
        exchanged.append(passed)
        if k + 4 < count:
            got[k + 4] = (passed, 0)
        go_round([k + 4], k + 3, *arrived(leaf_at, k + 2))
        wide = wides[k]
        at_leaf = [(owns[k], 0), got[k]]
        at_leaf += [(passed, low + i * wide) for i in range(2 * (n_pairs - 1))]
        pieces = woven((owns[k], 0), got[k], hub_at[k], leaf_at[k]), at_leaf
        done = parts[: max(0, k - 2 + (k + 1 == count))][-2:]
        base, before = 0, computed[-1:] + done
        if k == count - 2:
            early = product(
                is_hub, (after(beside_tokens, *before), own_tokens), wides[-1],
                *[[(owns[-1], 0), got[count - 1]]] * 2, (jnp.float32, jnp.float32),
            )
            before = early[1:]
        if k == count - 1:
            base, pieces = 2, [p[2:] for p in pieces]
        theirs, mine = product(
            is_hub, (after(beside_tokens, *before), own_tokens), wide, *pieces,
            (jnp.float32 if k == with_kv else jnp.bfloat16, jnp.float32), base,
            early if base else (),
        )
        if k == with_kv:
            other_kv = send(theirs[:, widths[k] :], across)
            theirs = theirs[:, : widths[k]].astype(jnp.bfloat16)
        other = send(theirs, across)
        if k == with_kv:
            kv = mine[:, widths[k] :] + other_kv
            mine = mine[:, : widths[k]]
            keys = norm_rope(
                kv[:, :HD], k_gain, own_tables[:, :HD], own_tables[:, HD : 2 * HD],
                lambda n: jnp.concatenate([n[:, HD // 2 :], n[:, : HD // 2]], axis=1),
            )
            keys_values = jnp.concatenate([keys, kv[:, HD:].astype(jnp.bfloat16)], axis=1)
        sums.append((mine, other))
        computed.append(mine)
        if keys is not None:
            while len(parts) < len(sums) - 1:
                parts.append(
                    attend(*sums[len(parts)], keys_values, own_tables, q_gain[None, :])
                )
    last, other = sums[-1]
    parts.append(attend(after(last, *parts[-1:]), other, keys_values, own_tables, q_gain[None, :]))
    return jnp.concatenate(parts, axis=1)


def solution(mesh):
    placed = (P("dp", None), P("dp", "head"), P("dp", "head"), P(), P(), P())
    return jax.shard_map(
        shards, mesh=mesh, in_specs=placed, out_specs=P("dp", "head"), check_vma=False
    )
```
